32 devices in a mesh: atom: 8 (over z, y), dp: 4 (over x, core).
Axes of the slice: x: 2, y: 2, z: 4, core: 2. Of those that a mesh axis runs over, the one named last changes fastest.
Arguments:
- activations: bfloat16 [512, 8192], P('dp'), may hold values from -6 to 6
- dictionary: bfloat16 [8192, 65536], P('dp', 'atom'), may hold values from -0.03535534 to 0.03535534
Outputs:
- sparse_codes: float32 [512, 65536], P('dp', 'atom')
- residual: float32 [512, 8192], P('atom', 'dp')
- new_dictionary: bfloat16 [8192, 65536], P('dp', 'atom')
The draws below stay inside these ranges and needn't reach their ends.
All inputs are finite; a program needn't handle non-finite values.
Results may differ from the reference program's by a relative error of at most 0.0025.
Values may be sent and summed in bfloat16 or wider, within the bound.
A program may use at most 256 MiB of HBM per device.

```python
import math
import jax
import jax.numpy as jnp
from jax import lax

D = 8192
ATOMS = 65536
ITERS = 2
ROWS = 512


def draw_dictionary(key, part):
    keys = jax.random.split(jax.random.fold_in(key, 11), 3)
    base = jax.random.truncated_normal(keys[0], -4.0, 4.0, (D, ATOMS), jnp.float32)
    feature_pos = jnp.arange(D, dtype=jnp.float32) / float(max(D - 1, 1))
    row_scale = 10.0 ** jax.random.uniform(keys[1], (D, 1), jnp.float32) * jnp.sqrt(1.0 + 2.0 * feature_pos)[:, None]
    col_scale = 10.0 ** jax.random.uniform(keys[2], (1, ATOMS), jnp.float32)
    return (base * row_scale * col_scale * 0.0046 / jnp.sqrt(float(D))).astype(jnp.bfloat16)


def level_of(stream_key, extent, pieces, least, top_value):
    gain, own = 1.0, jax.random.fold_in(stream_key, 6)
    for axis_at, shards_of in pieces:
        steps = jnp.exp(jax.random.uniform(jax.random.fold_in(own, axis_at), (shards_of,), jnp.float32, least / len(pieces), top_value / len(pieces)))
        gain = gain * jnp.repeat(steps, extent[axis_at] // shards_of).reshape([-1 if axis == axis_at else 1 for axis in range(len(extent))])
    return gain


def scatter_about(key, extent, scale, limit, cuts=(), held_as=jnp.bfloat16):
    loudness = level_of(key, extent, cuts, -0.22, 0.18) if cuts else 1.0
    result = jax.random.normal(key, extent, jnp.float32) * scale * loudness
    return jnp.minimum(jnp.maximum(result, -limit), limit).astype(held_as)


def setup_inputs(seed: int = 0) -> dict:
    arg_keys = jax.random.split(jax.random.key(seed), 3)
    activations = scatter_about(arg_keys[0], (ROWS, D), 1.0, 6.0, ((0, 4),))
    dictionary = draw_dictionary(jax.random.fold_in(arg_keys[2], 71), 0)
    return dict(activations=activations, dictionary=dictionary)


threshold = 0.05
step_size = 2.0
learn_rate = 1.0 / 16384.0
epsilon = 1e-12

def shrink(values):
    return values - jnp.clip(values, -threshold, threshold)

def product(left, right):
    return jnp.dot(left.astype(jnp.float32), right.astype(jnp.float32), precision=lax.Precision.HIGHEST, preferred_element_type=jnp.float32)

def residual_of(inputs, coded, dict_wide):
    recon = product(coded, dict_wide.T)
    full_residual = inputs - recon
    return (full_residual.astype(jnp.bfloat16), full_residual)

def reference(activations, dictionary):
    inputs = activations.astype(jnp.float32)
    dict_wide = dictionary.astype(jnp.float32)
    sparse_codes = jnp.zeros((ROWS, ATOMS), jnp.float32)
    rounded = activations
    coded = None
    for iteration in range(ITERS):
        if iteration > 0:
            rounded, residual = residual_of(inputs, coded, dict_wide)
        drive_term = product(rounded, dict_wide)
        sparse_codes = shrink(sparse_codes + step_size * drive_term)
        coded = sparse_codes.astype(jnp.bfloat16)
    rounded, residual = residual_of(inputs, coded, dict_wide)
    block_size = math.gcd(ATOMS, 4096)
    block_count = ATOMS // block_size
    weight_blocks = dictionary.reshape(D, block_count, block_size).transpose(1, 0, 2)
    code_blocks = coded.reshape(ROWS, block_count, block_size).transpose(1, 0, 2)
    rounded_t = rounded.T

    def update(blocks_pair):
        weight_block, code_block = blocks_pair
        gradient = product(rounded_t, code_block)
        shifted = weight_block.astype(jnp.float32) + learn_rate * gradient
        mean_square = lax.optimization_barrier(jnp.mean(shifted * shifted, axis=0))
        return (shifted * lax.rsqrt(mean_square + epsilon)).astype(jnp.bfloat16)
    updated = lax.map(update, (weight_blocks, code_blocks))
    new_dictionary = updated.transpose(1, 0, 2).reshape(D, ATOMS)
    return (sparse_codes, residual, new_dictionary)
```

```python
import jax
import jax.numpy as jnp
from jax import lax
from jax.sharding import PartitionSpec as P

ITERS = 2
CHUNKS = 2

threshold = 0.05
step_size = 2.0
learn_rate = 1.0 / 16384.0
epsilon = 1e-12


def shrink(values):
    return values - jnp.clip(values, -threshold, threshold)


def bits_of(count):
    return count.bit_length() - 1


def swap(value, axis, distance):
    pairs = [(i, i ^ distance) for i in range(lax.axis_size(axis))]
    return lax.ppermute(value, axis, pairs)


def body(activations, dictionary):
    n_dp, n_atom = lax.axis_size("dp"), lax.axis_size("atom")
    me_dp, me_atom = lax.axis_index("dp"), lax.axis_index("atom")
    per_owner = n_atom // n_dp
    features, atoms = dictionary.shape
    total_features = features * n_dp
    row_count = activations.shape[0]
    piece = row_count // (per_owner * CHUNKS)
    dp_bits, atom_bits = bits_of(n_dp), bits_of(n_atom)

    turn = me_atom ^ (me_dp * per_owner)
    turned = [((turn >> b) & 1) for b in range(atom_bits)]
    own_rows = activations.reshape(per_owner, CHUNKS, piece, total_features)

    def features_of(chunk):
        rows = own_rows[:, chunk].reshape(per_owner * piece, total_features)
        parts = []
        for p in range(n_dp):
            start = (me_dp ^ p) * features
            part = lax.dynamic_slice_in_dim(rows, start, features, 1)
            parts.append(part if p == 0 else swap(part, "dp", p))
        return jnp.concatenate(parts, axis=0)

    def sum_over_dp(partial):
        total = partial
        for b in range(dp_bits):
            view = total.reshape(-1, 2, per_owner * piece, atoms)
            kept, sent = view[:, 0], view[:, 1]
            if b > 0:
                sent = sent.astype(jnp.bfloat16)
            total = kept + swap(sent, "dp", 1 << b).astype(jnp.float32)
        return total.reshape(per_owner * piece, atoms)

    def gather_over_dp(own):
        gathered = own.reshape(1, per_owner * piece, atoms)
        for b in reversed(range(dp_bits)):
            other = swap(gathered, "dp", 1 << b)
            gathered = jnp.stack([gathered, other], axis=1).reshape(-1, per_owner * piece, atoms)
        return gathered.reshape(-1, atoms)

    def sum_over_atom(partial):
        total = partial
        for b in range(atom_bits):
            view = total.reshape(-1, 2, piece, features)
            kept = lax.dynamic_index_in_dim(view, turned[b], 1, keepdims=False)
            sent = lax.dynamic_index_in_dim(view, 1 - turned[b], 1, keepdims=False)
            sent = sent.astype(jnp.bfloat16)
            total = kept + swap(sent, "atom", 1 << b).astype(jnp.float32)
        return total.reshape(piece, features)

    def gather_over_atom(own):
        gathered = own.reshape(1, piece, features)
        for b in reversed(range(atom_bits)):
            other = swap(gathered, "atom", 1 << b)
            first = jnp.where(turned[b] == 0, gathered, other)
            second = jnp.where(turned[b] == 0, other, gathered)
            gathered = jnp.stack([first, second], axis=1).reshape(-1, piece, features)
        return gathered.reshape(-1, features)

    inputs = [features_of(chunk) for chunk in range(CHUNKS)]
    own_inputs = [
        lax.dynamic_index_in_dim(
            rows.reshape(n_atom, piece, features), turn, 0, keepdims=False
        ).astype(jnp.float32)
        for rows in inputs
    ]
    rounded = list(inputs)
    codes = [None] * CHUNKS
    coded = [None] * CHUNKS
    residual = [None] * CHUNKS
    for _ in range(ITERS):
        for c in range(CHUNKS):
            partial = jnp.dot(rounded[c], dictionary, preferred_element_type=jnp.float32)
            drive = step_size * sum_over_dp(partial)
            codes[c] = shrink(drive if codes[c] is None else codes[c] + drive)
            coded[c] = gather_over_dp(codes[c].astype(jnp.bfloat16))
            recon = lax.dot_general(
                coded[c], dictionary, (((1,), (1,)), ((), ())), preferred_element_type=jnp.float32
            )
            residual[c] = own_inputs[c] - sum_over_atom(recon)
            rounded[c] = gather_over_atom(residual[c].astype(jnp.bfloat16))

    all_rounded = jnp.concatenate(rounded, axis=0)
    all_coded = jnp.concatenate(coded, axis=0)

    def moved(left, right):
        gradient = lax.dot_general(
            left, right, (((0,), (0,)), ((), ())), preferred_element_type=jnp.float32
        )
        return dictionary.astype(jnp.float32) + learn_rate * gradient

    first = moved(all_rounded, all_coded)
    squares = lax.psum(jnp.sum(first * first, axis=0), "dp")
    again_rounded, again_coded, squares = lax.optimization_barrier((all_rounded, all_coded, squares))
    scale = lax.rsqrt(squares / total_features + epsilon)
    new_dictionary = (moved(again_rounded, again_coded) * scale).astype(jnp.bfloat16)

    sparse_codes = jnp.stack(
        [value.reshape(per_owner, piece, atoms) for value in codes], axis=1
    ).reshape(row_count, atoms)
    return (sparse_codes, jnp.concatenate(residual, axis=0), new_dictionary)


def solution(mesh):
    placed = (P("dp", None), P("dp", "atom"))
    return jax.shard_map(
        body,
        mesh=mesh,
        in_specs=placed,
        out_specs=(P("dp", "atom"), P("atom", "dp"), P("dp", "atom")),
        check_vma=False,
    )
```

```python
import jax
import jax.numpy as jnp
from jax import lax
from jax.sharding import PartitionSpec as P

ITERS = 2
CHUNKS = 2

threshold = 0.05
step_size = 2.0
learn_rate = 1.0 / 16384.0
epsilon = 1e-12


def shrink(values):
    return values - jnp.clip(values, -threshold, threshold)


def bits_of(count):
    return count.bit_length() - 1


def swap(value, axis, distance):
    pairs = [(i, i ^ distance) for i in range(lax.axis_size(axis))]
    return lax.ppermute(value, axis, pairs)


def body(activations, dictionary):
    n_dp, n_atom = lax.axis_size("dp"), lax.axis_size("atom")
    me_dp, me_atom = lax.axis_index("dp"), lax.axis_index("atom")
    per_owner = n_atom // n_dp
    features, atoms = dictionary.shape
    total_features = features * n_dp
    row_count = activations.shape[0]
    piece = row_count // (per_owner * CHUNKS)
    dp_bits, atom_bits = bits_of(n_dp), bits_of(n_atom)

    turn = me_atom ^ (me_dp * per_owner)
    turned = [((turn >> b) & 1) for b in range(atom_bits)]
    own_rows = activations.reshape(per_owner, CHUNKS, piece, total_features)

    def after(value, done):
        return value if done is None else lax.optimization_barrier((value, done))[0]

    last = []

    def after_last(value):
        if last:
            value = after(value, last.pop())
        return value

    def features_of(chunk, done):
        rows = own_rows[:, chunk].reshape(per_owner * piece, total_features)
        rows = after(rows, done)
        parts = []
        for p in range(n_dp):
            start = (me_dp ^ p) * features
            part = lax.dynamic_slice_in_dim(rows, start, features, 1)
            parts.append(part if p == 0 else swap(part, "dp", p))
        return jnp.concatenate(parts, axis=0)

    def halve(total):
        view = total.reshape(-1, 2, per_owner * piece, atoms)
        return view[:, 0], view[:, 1]

    def sum_first(partial):
        kept, sent = halve(partial)
        return kept + swap(sent, "dp", 1)

    def sum_rest(total):
        for b in range(1, dp_bits):
            kept, sent = halve(total)
            other = swap(after_last(sent.astype(jnp.bfloat16)), "dp", 1 << b)
            last[:] = [other]
            total = kept + other.astype(jnp.float32)
        return total.reshape(per_owner * piece, atoms)

    def gather_over_dp(own, before_chips, before_cores):
        gathered = after(own, before_chips).reshape(1, per_owner * piece, atoms)
        for b in reversed(range(dp_bits)):
            if b > 0:
                gathered = after_last(gathered)
            else:
                gathered = after(gathered, before_cores)
            other = swap(gathered, "dp", 1 << b)
            if b > 0:
                last[:] = [other]
            gathered = jnp.stack([gathered, other], axis=1).reshape(-1, per_owner * piece, atoms)
        return gathered.reshape(-1, atoms)

    def sum_over_atom(partial, before):
        total = partial
        for b in range(atom_bits):
            view = total.reshape(-1, 2, piece, features)
            kept = lax.dynamic_index_in_dim(view, turned[b], 1, keepdims=False)
            sent = lax.dynamic_index_in_dim(view, 1 - turned[b], 1, keepdims=False)
            sent = sent.astype(jnp.bfloat16)
            if b == 0:
                sent = after(sent, before)
            total = kept + swap(sent, "atom", 1 << b).astype(jnp.float32)
        return total.reshape(piece, features)

    def gather_over_atom(own):
        gathered = own.reshape(1, piece, features)
        for b in reversed(range(atom_bits)):
            other = swap(gathered, "atom", 1 << b)
            first = jnp.where(turned[b] == 0, gathered, other)
            second = jnp.where(turned[b] == 0, other, gathered)
            gathered = jnp.stack([first, second], axis=1).reshape(-1, piece, features)
        return gathered.reshape(-1, features)

    inputs = []
    for chunk in range(CHUNKS):
        inputs.append(features_of(chunk, inputs[-1] if inputs else None))
    own_inputs = [
        lax.dynamic_index_in_dim(
            rows.reshape(n_atom, piece, features), turn, 0, keepdims=False
        ).astype(jnp.float32)
        for rows in inputs
    ]
    rounded = list(inputs)
    codes = [None] * CHUNKS
    coded = [None] * CHUNKS
    residual = [None] * CHUNKS

    def drive_of(rows):
        return jnp.dot(rows, dictionary, preferred_element_type=jnp.float32)

    summed = [sum_first(drive_of(rows)) for rows in inputs]
    recon = driven = None
    total = sum_rest(summed[0])
    for step in range(ITERS):
        for c in range(CHUNKS):
            drive = step_size * total
            codes[c] = shrink(drive if codes[c] is None else codes[c] + drive)
            coded[c] = gather_over_dp(codes[c].astype(jnp.bfloat16), recon, driven)
            arrived = None
            if step + 1 < ITERS or c + 1 < CHUNKS:
                following = summed[(c + 1) % CHUNKS]
                total = sum_rest(following)
                coded[c] = after(coded[c], following)
                arrived = last[0] if last else None
            recon = lax.dot_general(
                coded[c], dictionary, (((1,), (1,)), ((), ())), preferred_element_type=jnp.float32
            )
            residual[c] = own_inputs[c] - sum_over_atom(recon, arrived)
            rounded[c] = gather_over_atom(residual[c].astype(jnp.bfloat16))
            driven = None
            if step + 1 < ITERS:
                driven = drive_of(rounded[c])
                summed[c] = sum_first(driven)

    all_rounded = jnp.concatenate(rounded, axis=0)
    all_coded = jnp.concatenate(coded, axis=0)

    def moved(left, right):
        gradient = lax.dot_general(
            left, right, (((0,), (0,)), ((), ())), preferred_element_type=jnp.float32
        )
        return dictionary.astype(jnp.float32) + learn_rate * gradient

    first = moved(all_rounded, all_coded)
    squares = lax.psum(jnp.sum(first * first, axis=0), "dp")
    again_rounded, again_coded, squares = lax.optimization_barrier((all_rounded, all_coded, squares))
    scale = lax.rsqrt(squares / total_features + epsilon)
    new_dictionary = (moved(again_rounded, again_coded) * scale).astype(jnp.bfloat16)

    sparse_codes = jnp.stack(
        [value.reshape(per_owner, piece, atoms) for value in codes], axis=1
    ).reshape(row_count, atoms)
    return (sparse_codes, jnp.concatenate(residual, axis=0), new_dictionary)


def solution(mesh):
    placed = (P("dp", None), P("dp", "atom"))
    return jax.shard_map(
        body,
        mesh=mesh,
        in_specs=placed,
        out_specs=(P("dp", "atom"), P("atom", "dp"), P("dp", "atom")),
        check_vma=False,
    )
```

```python
import jax
import jax.numpy as jnp
from jax import lax
from jax.sharding import PartitionSpec as P

ITERS = 2
CHUNKS = 2

threshold = 0.05
step_size = 2.0
learn_rate = 1.0 / 16384.0
epsilon = 1e-12


def shrink(values):
    return values - jnp.clip(values, -threshold, threshold)


def bits_of(count):
    return count.bit_length() - 1


def swap(value, axis, distance):
    pairs = [(i, i ^ distance) for i in range(lax.axis_size(axis))]
    return lax.ppermute(value, axis, pairs)


def body(activations, dictionary):
    n_dp, n_atom = lax.axis_size("dp"), lax.axis_size("atom")
    me_dp, me_atom = lax.axis_index("dp"), lax.axis_index("atom")
    per_owner = n_atom // n_dp
    features, atoms = dictionary.shape
    total_features = features * n_dp
    row_count = activations.shape[0]
    piece = row_count // (per_owner * CHUNKS)
    dp_bits, atom_bits = bits_of(n_dp), bits_of(n_atom)

    turn = me_atom ^ (me_dp * per_owner)
    turned = [((turn >> b) & 1) for b in range(atom_bits)]
    own_rows = activations.reshape(per_owner, CHUNKS, piece, total_features)

    def after(value, done):
        return value if done is None else lax.optimization_barrier((value, done))[0]

    last = []

    def after_last(value):
        if last:
            value = after(value, last.pop())
        return value

    def features_of(chunk, done):
        rows = own_rows[:, chunk].reshape(per_owner * piece, total_features)
        rows = after(rows, done)
        parts = []
        for p in range(n_dp):
            start = (me_dp ^ p) * features
            part = lax.dynamic_slice_in_dim(rows, start, features, 1)
            parts.append(part if p == 0 else swap(part, "dp", p))
        return jnp.concatenate(parts, axis=0)

    def halve(total):
        view = total.reshape(-1, 2, per_owner * piece, atoms)
        return view[:, 0], view[:, 1]

    def sum_first(partial):
        kept, sent = halve(partial)
        return kept + swap(sent, "dp", 1)

    def sum_rest(total):
        for b in range(1, dp_bits):
            kept, sent = halve(total)
            other = swap(after_last(sent.astype(jnp.bfloat16)), "dp", 1 << b)
            last[:] = [other]
            total = kept + other.astype(jnp.float32)
        return total.reshape(per_owner * piece, atoms)

    def gather_over_dp(own, before_chips, before_cores):
        gathered = after(own, before_chips).reshape(1, per_owner * piece, atoms)
        for b in reversed(range(dp_bits)):
            if b > 0:
                gathered = after_last(gathered)
            else:
                gathered = after(gathered, before_cores)
            other = swap(gathered, "dp", 1 << b)
            if b > 0:
                last[:] = [other]
            gathered = jnp.stack([gathered, other], axis=1).reshape(-1, per_owner * piece, atoms)
        return gathered.reshape(-1, atoms)

    def sum_over_atom(partial, before):
        total = partial
        for b in range(atom_bits):
            view = total.reshape(-1, 2, piece, features)
            kept = lax.dynamic_index_in_dim(view, turned[b], 1, keepdims=False)
            sent = lax.dynamic_index_in_dim(view, 1 - turned[b], 1, keepdims=False)
            sent = sent.astype(jnp.bfloat16)
            if b == 0:
                sent = after(sent, before)
            total = kept + swap(sent, "atom", 1 << b).astype(jnp.float32)
        return total.reshape(piece, features)

    def gather_over_atom(own):
        gathered = own.reshape(1, piece, features)
        for b in reversed(range(atom_bits)):
            other = swap(gathered, "atom", 1 << b)
            first = jnp.where(turned[b] == 0, gathered, other)
            second = jnp.where(turned[b] == 0, other, gathered)
            gathered = jnp.stack([first, second], axis=1).reshape(-1, piece, features)
        return gathered.reshape(-1, features)

    inputs = []
    for chunk in range(CHUNKS):
        inputs.append(features_of(chunk, None))
    own_inputs = [
        lax.dynamic_index_in_dim(
            rows.reshape(n_atom, piece, features), turn, 0, keepdims=False
        ).astype(jnp.float32)
        for rows in inputs
    ]
    rounded = list(inputs)
    codes = [None] * CHUNKS
    coded = [None] * CHUNKS
    residual = [None] * CHUNKS

    def drive_of(rows):
        return jnp.dot(rows, dictionary, preferred_element_type=jnp.float32)

    summed = [sum_first(drive_of(rows)) for rows in inputs]
    recon = driven = None
    total = sum_rest(summed[0])
    for step in range(ITERS):
        for c in range(CHUNKS):
            drive = step_size * total
            codes[c] = shrink(drive if codes[c] is None else codes[c] + drive)
            coded[c] = gather_over_dp(codes[c].astype(jnp.bfloat16), recon, driven)
            arrived = None
            if step + 1 < ITERS or c + 1 < CHUNKS:
                following = summed[(c + 1) % CHUNKS]
                total = sum_rest(following)
                coded[c] = after(coded[c], following)
                arrived = last[0] if last else None
            recon = lax.dot_general(
                coded[c], dictionary, (((1,), (1,)), ((), ())), preferred_element_type=jnp.float32
            )
            residual[c] = own_inputs[c] - sum_over_atom(recon, arrived)
            rounded[c] = gather_over_atom(residual[c].astype(jnp.bfloat16))
            driven = None
            if step + 1 < ITERS:
                driven = drive_of(rounded[c])
                summed[c] = sum_first(driven)

    all_rounded = jnp.concatenate(rounded, axis=0)
    all_coded = jnp.concatenate(coded, axis=0)

    def moved(left, right):
        gradient = lax.dot_general(
            left, right, (((0,), (0,)), ((), ())), preferred_element_type=jnp.float32
        )
        return dictionary.astype(jnp.float32) + learn_rate * gradient

    first = moved(all_rounded, all_coded)
    squares = lax.psum(jnp.sum(first * first, axis=0), "dp")
    again_rounded, again_coded, squares = lax.optimization_barrier((all_rounded, all_coded, squares))
    scale = lax.rsqrt(squares / total_features + epsilon)
    new_dictionary = (moved(again_rounded, again_coded) * scale).astype(jnp.bfloat16)

    sparse_codes = jnp.stack(
        [value.reshape(per_owner, piece, atoms) for value in codes], axis=1
    ).reshape(row_count, atoms)
    return (sparse_codes, jnp.concatenate(residual, axis=0), new_dictionary)


def solution(mesh):
    placed = (P("dp", None), P("dp", "atom"))
    return jax.shard_map(
        body,
        mesh=mesh,
        in_specs=placed,
        out_specs=(P("dp", "atom"), P("atom", "dp"), P("dp", "atom")),
        check_vma=False,
    )
```
